32 devices in a mesh: row: 2 (over x), col: 4 (over y, core), layer: 4 (over z).
Axes of the slice: x: 2, y: 2, z: 4, core: 2. Of those that a mesh axis runs over, the one named last changes fastest.
Arguments:
- amplitudes: bfloat16 [2, 4, 128, 8192], P('row', 'col', None, 'layer'), may hold values from -6 to 6
- tile_mask: int32 [2, 4, 128, 32], P('row', 'col', None, 'layer'), may hold values 0 or 1
- owners: int32 [2, 4, 128, 1], P('row', 'col'), may hold values from 0 to 7; in each aligned block of 128 rows (0 to 127, 128 to 255, ..., all dimensions but the last counted through in order) at most 32 rows name the same one
- col_panels: bfloat16 [2, 4, 4, 256, 512], P('row', 'col', 'layer'), may hold values from -0.0625 to 0.0625
- row_panels: bfloat16 [2, 4, 4, 256, 512], P('row', 'col', 'layer'), may hold values from -0.0625 to 0.0625
Outputs:
- residual: bfloat16 [2, 4, 128, 512], P('row', 'col', None, 'layer')
The draws below stay inside these ranges and needn't reach their ends.
Inputs may be any that keep to these rules, and one draw needn't show every extreme that they name: `owners`: among the 128 rows of one grid position at most 32 name the same destination, and in every draw some grid position names one destination exactly 32 times.
All inputs are finite; a program needn't handle non-finite values. No bound on the sum of `tile_mask` on one device may be relied on, other than what follows from the above.
Results may differ from the reference program's by a relative error of at most 0.013.
Values may be sent and summed in bfloat16 or wider, within the bound.
A program may use at most 64 MiB of HBM per device.

```python
import math
import jax
import jax.numpy as jnp
import numpy as np
from jax import lax

TW = 256
STEPS = 4
ROWS_DEV = 128
KW = 2048
NW = 512
CAP = 32
N_ROW = 2
N_COL = 4
N_LAYER = 4


def place_ends(entries, key, low, largest):
    spot = [jax.random.randint(jax.random.fold_in(key, axis), (), 0, length) for axis, length in enumerate(entries.shape)]
    longest = entries.shape.index(max(entries.shape))
    beside = spot[:longest] + [(spot[longest] + 1) % entries.shape[longest]] + spot[longest + 1:]
    return entries.at[tuple(spot)].set(low).at[tuple(beside)].set(largest)


def shard_levels(key, extent, cuts, smallest, high):
    def one(axis_at, shards_of):
        draws = jax.random.uniform(jax.random.fold_in(jax.random.fold_in(key, 6), axis_at), (shards_of,), jnp.float32, smallest / len(cuts), high / len(cuts))
        return jnp.repeat(jnp.exp(draws), extent[axis_at] // shards_of).reshape((-1,) + (1,) * (len(extent) - axis_at - 1))

    loudness = one(*cuts[0])
    for cut in cuts[1:]:
        loudness = loudness * one(*cut)
    return loudness


def deal_out(rng, own, number, rows, number_of, top, most, slope):
    ranking = jax.random.permutation(rng, number_of)
    heavy_load, ordinary = portions_of(number_of, rows * top, most, slope, True), portions_of(number_of, rows * top, most, slope, False)
    places = jnp.arange(number_of)

    def named(tallies, offset_by):
        used = int((tallies > 0).sum())
        fixed = max(1, used // 4)
        passed = fixed + (places - fixed + offset_by * (used - fixed)) % max(1, number_of - fixed)
        return jnp.zeros((number_of,), jnp.int32).at[ranking[jnp.where(places < fixed, places, passed)]].set(jnp.asarray(tallies, jnp.int32))

    tallies = jnp.where(number % 4 == 0, named(heavy_load, number // 4), named(ordinary, number - number // 4 - 1))
    mixed = jax.random.permutation(jax.random.fold_in(own, 3), number_of)
    source_of, taker = mixed[0:number_of // 2 * 2:2], mixed[1:number_of // 2 * 2:2]
    room = jnp.minimum(tallies[source_of] - 1, most - tallies[taker]) // 2
    room = jnp.where((source_of == ranking[0]) | (taker == ranking[0]) | (tallies[taker] == 0), 0, jnp.maximum(room, 0))
    passed = jax.random.randint(jax.random.fold_in(own, 4), (number_of // 2,), 0, 1 << 20) % (room + 1)
    tallies = tallies.at[source_of].add(-passed).at[taker].add(passed)
    labels = jnp.searchsorted(jnp.cumsum(tallies), jnp.arange(rows * top), side="right").astype(jnp.int32)
    listing = labels.reshape(top, rows).T
    listing = listing[jax.random.permutation(jax.random.fold_in(own, 1), rows)]
    offset_by = jax.random.randint(jax.random.fold_in(own, 2), (rows, 1), 0, top)
    return jnp.take_along_axis(listing, (jnp.arange(top)[None, :] + offset_by) % top, axis=1)


def portions_of(amount, total, most, lean, full):
    portions = [(1 << 20) // math.isqrt(standing ** lean) + 1 for standing in range(1, amount + 1)]
    largest = most if full else min(most, max(-(-total // amount), total * portions[0] // sum(portions)))
    least = 1 if total - largest >= amount - 1 else 0
    counts, surplus = [largest] + [least] * (amount - 1), total - largest - least * (amount - 1)
    while surplus > 0:
        candidates = [i for i in range(1, amount) if counts[i] < largest] or [i for i in range(1, amount) if counts[i] < most]
        whole, budget = sum([portions[i] for i in candidates]), surplus
        for i in candidates:
            more = min(most - counts[i], max(1, budget * portions[i] // whole), surplus)
            counts[i] = counts[i] + more
            surplus = surplus - more
    return np.array(counts)


def bell_draw(rng, extent, deviation, most, shards=(), kind=jnp.bfloat16):
    entries = jax.random.normal(rng, extent, jnp.float32) * deviation
    if len(shards) > 0:
        entries = shard_levels(rng, extent, shards, -0.22, 0.18) * entries
    return jnp.clip(entries, min=-most, max=most).astype(kind)


def setup_inputs(seed: int = 0) -> dict:
    splits = jax.random.split(jax.random.key(seed), 6)
    amplitudes = bell_draw(splits[0], (N_ROW, N_COL, ROWS_DEV, N_LAYER * KW), 1.0, 6.0, ((0, 2), (1, 4), (3, 4)))
    tile_mask = place_ends((jax.random.randint(splits[1], (N_ROW, N_COL, ROWS_DEV, N_LAYER * 2 * STEPS), 0, 4) < 3).astype(jnp.int32), jax.random.fold_in(splits[1], 1), 0, 1)
    owners_keys = jax.random.split(jax.random.fold_in(splits[2], 1), N_ROW * N_COL * ROWS_DEV // ROWS_DEV)
    owners_turns = jax.random.permutation(jax.random.fold_in(splits[2], 3), N_ROW * N_COL * ROWS_DEV // ROWS_DEV)
    owners = jax.vmap(lambda own, number: deal_out(jax.random.fold_in(splits[2], 2), own, number, ROWS_DEV, N_ROW * N_COL, 1, CAP, 2))(owners_keys, owners_turns).reshape((N_ROW, N_COL, ROWS_DEV, 1))
    col_panels = bell_draw(splits[3], (N_ROW, N_COL, N_LAYER, TW, NW), (KW * N_LAYER) ** -0.5, 0.0625, ((0, 2), (1, 4), (2, 4)))
    row_panels = bell_draw(splits[4], (N_ROW, N_COL, N_LAYER, TW, NW), (KW * N_LAYER) ** -0.5, 0.0625, ((0, 2), (1, 4), (2, 4)))
    return dict(amplitudes=amplitudes, tile_mask=tile_mask, owners=owners, col_panels=col_panels, row_panels=row_panels)


def reference(amplitudes, tile_mask, owners, col_panels, row_panels):
    grid_rows, grid_cols, rows_here, full_width = amplitudes.shape
    layers = col_panels.shape[2]
    tile_width = col_panels.shape[3]
    panel_width = col_panels.shape[4]
    peer_count = grid_rows * grid_cols
    capacity = CAP
    blocks = tile_mask.shape[3]
    flat_amp = amplitudes.reshape(peer_count * rows_here, blocks, tile_width)
    flat_mask = tile_mask.reshape(peer_count * rows_here, blocks)
    destined = owners.reshape(peer_count, rows_here).astype(jnp.int32)
    targets = jnp.arange(peer_count, dtype=jnp.int32)
    onehot = (destined[:, :, None] == targets[None, None, :]).astype(jnp.int32)
    slot_rank = jnp.sum((jnp.cumsum(onehot, axis=1) - onehot) * onehot, axis=2).astype(jnp.int32)
    sources = jnp.broadcast_to(targets[:, None], (peer_count, rows_here))
    flat_slot = ((destined * peer_count + sources) * capacity + slot_rank).astype(jnp.int32)
    row_ids = jnp.arange(peer_count * rows_here, dtype=jnp.int32)
    table = jnp.full((peer_count * peer_count * capacity,), -1, jnp.int32).at[flat_slot.reshape(-1)].set(row_ids)
    table = table.reshape(peer_count, peer_count * capacity)

    def one_dest(inputs):
        index, dest = inputs
        valid = index >= 0
        safe_index = jnp.maximum(index, 0)
        keep_mask = jnp.where(valid[:, None], jnp.take(flat_mask, safe_index, axis=0), 0).astype(amplitudes.dtype)
        gathered = jnp.take(flat_amp, safe_index, axis=0) * keep_mask[:, :, None]
        gathered = gathered.astype(jnp.float32)
        dest_row = dest // grid_cols
        dest_col = dest % grid_cols
        total = jnp.zeros((index.shape[0], panel_width), jnp.float32)
        for layer in range(layers):
            part = jnp.zeros((index.shape[0], panel_width), jnp.float32)
            base = layer * 2 * STEPS
            for position in range(STEPS):
                col_panel = col_panels[dest_row, (dest_col + position) % grid_cols, layer].astype(jnp.float32)
                row_panel = row_panels[(dest_row + position) % grid_rows, dest_col, layer].astype(jnp.float32)
                part = part + jnp.dot(gathered[:, base + position], col_panel, preferred_element_type=jnp.float32)
                part = part + jnp.dot(gathered[:, base + STEPS + position], row_panel, preferred_element_type=jnp.float32)
            rounded = lax.optimization_barrier(part.astype(jnp.bfloat16))
            total = total + rounded.astype(jnp.float32)
        return total.astype(jnp.bfloat16)

    per_dest = lax.map(one_dest, (table, targets))
    result = per_dest[destined, sources * capacity + slot_rank]
    return result.reshape(grid_rows, grid_cols, rows_here, panel_width)
```

```python
import functools

import jax
import jax.numpy as jnp
from jax import lax
from jax.experimental import pallas as pl
from jax.experimental.pallas import tpu as pltpu
from jax.sharding import PartitionSpec as P

MESH = pl.DeviceIdType.MESH
GROUPS = 2


def from_behind(x, axis, by):
    length = lax.axis_size(axis)
    return lax.ppermute(x, axis, [(i, (i + by) % length) for i in range(length)])


def routed(amplitudes, tile_mask, owners, col_panels, row_panels):
    rows_here = amplitudes.shape[2]
    width_k = amplitudes.shape[3]
    blocks = tile_mask.shape[3]
    tile_width = width_k // blocks
    half_blocks = blocks // 2
    grid_rows = lax.axis_size("row")
    grid_cols = lax.axis_size("col")
    peer_count = grid_rows * grid_cols
    capacity = max(2, 2 * rows_here // peer_count)
    slot_count = peer_count * capacity
    keep_mask = tile_mask[0, 0].astype(jnp.bfloat16)
    masked = (
        amplitudes[0, 0].reshape(rows_here, blocks, tile_width) * keep_mask[:, :, None]
    ).reshape(rows_here, width_k)
    destined = owners[0, 0, :, 0]
    ids = jnp.arange(rows_here, dtype=jnp.int32)
    earlier = (destined[:, None] == destined[None, :]) & (ids[None, :] < ids[:, None])
    slot_rank = jnp.sum(earlier.astype(jnp.int32), axis=1)
    slot_index = destined * capacity + slot_rank
    source_of = jnp.zeros((slot_count,), jnp.int32).at[slot_index].set(ids)
    filled = jnp.zeros((slot_count,), jnp.int32).at[slot_index].set(1)
    outgoing = jnp.take(masked, source_of, axis=0) * filled[:, None].astype(jnp.bfloat16)
    arrived = lax.all_to_all(
        outgoing.reshape(peer_count, capacity, width_k),
        ("row", "col"),
        split_axis=0,
        concat_axis=0,
        tiled=True,
    )
    arrived = arrived.reshape(slot_count, width_k)
    col_panel = col_panels[0, 0, 0]
    row_panel = row_panels[0, 0, 0]
    partial_value = jnp.zeros((slot_count, col_panel.shape[1]), jnp.float32)
    for position in range(half_blocks):
        if position > 0:
            col_panel = from_behind(col_panel, "col", -1)
            row_panel = from_behind(row_panel, "row", -1)
        col_block = arrived[:, position * tile_width : (position + 1) * tile_width]
        row_block = arrived[
            :, (half_blocks + position) * tile_width : (half_blocks + position + 1) * tile_width
        ]
        partial_value = partial_value + jnp.dot(
            col_block, col_panel, preferred_element_type=jnp.float32
        )
        partial_value = partial_value + jnp.dot(
            row_block, row_panel, preferred_element_type=jnp.float32
        )
    rounded = partial_value.astype(jnp.bfloat16)
    returned = lax.all_to_all(
        rounded.reshape(peer_count, capacity, rounded.shape[1]),
        ("row", "col"),
        split_axis=0,
        concat_axis=0,
        tiled=True,
    )
    own_rows = jnp.take(returned.reshape(slot_count, rounded.shape[1]), slot_index, axis=0)
    result = lax.psum_scatter(
        own_rows.astype(jnp.float32).astype(jnp.bfloat16), "layer", scatter_dimension=1, tiled=True
    )
    return result.reshape(1, 1, rows_here, result.shape[1])


def kernel(layers, amp, mask, own, colp, rowp, out, panels, lhs, xs, xr, outb, inbox,
           ysend, yrecv, ssend, srecv, fsend, frecv, xsend, xrecv, osend, irecv):
    rows, tw, nw = amp.shape[0], colp.shape[0], colp.shape[1]
    gw, cw = nw // GROUPS, nw // layers
    x, q, z = lax.axis_index("row"), lax.axis_index("col"), lax.axis_index("layer")
    core = lax.rem(q, 2)
    sib, yq = q + 1 - 2 * core, lax.rem(q + 2, 4)
    ysib = yq + 1 - 2 * core
    cols = [q, sib, yq, ysib]
    other = 1 - x

    barrier = pltpu.get_barrier_semaphore()

    def greet(device):
        pl.semaphore_signal(barrier, inc=1, device_id=device, device_id_type=MESH)

    greet((x, yq, z))
    greet((x, sib, z))
    for n in range(layers):
        greet((other, q, n))

        @pl.when(n != z)
        def _():
            greet((x, q, n))

    def copy(src, dst, s, r, device):
        return pltpu.make_async_remote_copy(
            src_ref=src, dst_ref=dst, send_sem=s, recv_sem=r, device_id=device, device_id_type=MESH
        )

    def group(g):
        return pl.ds(g * gw, gw)

    own_panels = [colp, rowp]
    to_y = [[copy(own_panels[k].at[:, group(g)], panels.at[k, 1, :, group(g)], ysend.at[k, g],
                  yrecv.at[k, g], (x, yq, z)) for k in range(2)] for g in range(GROUPS)]
    to_sib = [copy(own_panels[k], panels.at[k, 0], ssend.at[k], srecv.at[k], (x, sib, z))
              for k in range(2)]
    onward = [[copy(panels.at[k, 1, :, group(g)], panels.at[k, 2, :, group(g)], fsend.at[k, g],
                    frecv.at[k, g], (x, sib, z)) for k in range(2)] for g in range(GROUPS)]
    code_row = pl.ds(0, 128 + 2 * tw)
    to_x = [
        copy(xs.at[:, code_row], xr, xsend.at[0], xrecv.at[0], (other, q, z)),
        copy(xs.at[:, pl.ds(128 + 2 * tw, 4 * tw)], lhs.at[pl.ds(rows, rows), pl.ds(0, 4 * tw)],
             xsend.at[1], xrecv.at[1], (other, q, z)),
    ]

    def wide(a):
        return jnp.concatenate([a] * (tw // 128), axis=1)

    def flag(cond):
        return wide(cond.astype(jnp.float32).astype(jnp.bfloat16))

    dest = jnp.broadcast_to(own[...], (rows, 128))
    dest_row = jnp.where(dest >= 4, 1, 0)
    dest_col = dest - 4 * dest_row
    here, there = flag(dest_row == x), flag(dest_row != x)

    def block(m):
        keep = jnp.broadcast_to(mask[:, m : m + 1], (rows, 128))
        return amp[:, m * tw : (m + 1) * tw] * flag(keep != 0)

    xs[:, :128] = dest_col.astype(jnp.float32).astype(jnp.bfloat16)
    own_row = []
    for m in range(2):
        even, odd = block(4 + 2 * m), block(5 + 2 * m)
        own_row.append(even * here + odd * there)
        xs[:, 128 + m * tw : 128 + (m + 1) * tw] = odd * here + even * there
    col_blocks = [block(s) for s in range(4)]
    for j in range(4):
        met = sum(col_blocks[s] * flag(dest_col == lax.rem(cols[j] + 4 - s, 4)) for s in range(4))
        lhs[:rows, j * tw : (j + 1) * tw] = met * here
        xs[:, 128 + (2 + j) * tw : 128 + (3 + j) * tw] = met * there

    pl.semaphore_wait(barrier, 2 * layers + 1)
    for c in to_sib:
        c.start()
    for c in to_y[0]:
        c.start()
    for c in to_x:
        c.start()
    for g in range(1, GROUPS):
        for c in to_y[g]:
            c.start()

    for j in range(4):
        meets = flag(dest_col == cols[j])
        for m in range(2):
            lhs[:rows, (4 + 2 * j + m) * tw : (5 + 2 * j + m) * tw] = own_row[m] * meets

    for c in to_sib:
        c.wait_recv()
    for c in to_x:
        c.wait_recv()
    code = xr[:, :128].astype(jnp.float32)
    for j in range(4):
        meets = flag(code == cols[j].astype(jnp.float32))
        for m in range(2):
            lhs[rows:, (4 + 2 * j + m) * tw : (5 + 2 * j + m) * tw] = (
                xr[:, 128 + m * tw : 128 + (m + 1) * tw] * meets
            )

    def result(n, side):
        return copy(outb.at[side, n], inbox.at[z, side], osend.at[side, n], irecv.at[z, side],
                    (x if side == 0 else other, q, n))

    for g in range(GROUPS):
        for k in range(2):
            to_y[g][k].wait_recv()
            onward[g][k].start()
        total = jnp.zeros((2 * rows, gw), jnp.float32)
        for j in range(4):
            if j == 3:
                for k in range(2):
                    onward[g][k].wait_recv()
            col = colp[:, g * gw : (g + 1) * gw] if j == 0 else panels[0, j - 1, :, g * gw : (g + 1) * gw]
            row = rowp[:, g * gw : (g + 1) * gw] if j == 0 else panels[1, j - 1, :, g * gw : (g + 1) * gw]
            total += jnp.dot(lhs[:, j * tw : (j + 1) * tw], col, preferred_element_type=jnp.float32)
            for m in range(2):
                at = (4 + 2 * j + m) * tw
                total += jnp.dot(lhs[:, at : at + tw], row, preferred_element_type=jnp.float32)
        total = total.astype(jnp.bfloat16)
        for i in range(layers // GROUPS):
            n = g * (layers // GROUPS) + i
            outb[0, n] = total[:rows, i * cw : (i + 1) * cw]
            outb[1, n] = total[rows:, i * cw : (i + 1) * cw]
            result(n, 1).start()

            @pl.when(n != z)
            def _():
                result(n, 0).start()

            @pl.when(n == z)
            def _():
                inbox[n, 0] = outb[0, n]

    def arrived(n, side):
        copy(outb.at[side, n], inbox.at[n, side], osend.at[side, n], irecv.at[n, side],
             (x if side == 0 else other, q, n)).wait_recv()

    for n in range(layers):
        arrived(n, 1)

        @pl.when(n != z)
        def _():
            arrived(n, 0)

    result_sum = jnp.zeros((rows, cw), jnp.float32)
    for n in range(layers):
        result_sum += inbox[n, 0].astype(jnp.float32) + inbox[n, 1].astype(jnp.float32)
    out[...] = result_sum.astype(out.dtype)

    for c in to_sib + to_x:
        c.wait_send()
    for g in range(GROUPS):
        for c in to_y[g] + onward[g]:
            c.wait_send()
    for n in range(layers):
        result(n, 1).wait_send()

        @pl.when(n != z)
        def _():
            result(n, 0).wait_send()


def crossed(amplitudes, tile_mask, owners, col_panels, row_panels):
    layers = lax.axis_size("layer")
    rows, width_k = amplitudes.shape[2:]
    tw, nw = col_panels.shape[3:]
    blocks = tile_mask.shape[3]
    cw = nw // layers
    dma = pltpu.SemaphoreType.DMA
    bf16 = jnp.bfloat16
    vmem = pl.BlockSpec(memory_space=pltpu.VMEM)
    result = pl.pallas_call(
        functools.partial(kernel, layers),
        out_shape=jax.ShapeDtypeStruct((rows, cw), bf16),
        in_specs=[vmem] * 5,
        out_specs=vmem,
        scratch_shapes=[
            pltpu.VMEM((2, 3, tw, nw), bf16),
            pltpu.VMEM((2 * rows, 12 * tw), bf16),
            pltpu.VMEM((rows, 128 + 6 * tw), bf16),
            pltpu.VMEM((rows, 128 + 2 * tw), bf16),
            pltpu.VMEM((2, layers, rows, cw), bf16),
            pltpu.VMEM((layers, 2, rows, cw), bf16),
            dma((2, GROUPS)), dma((2, GROUPS)), dma((2,)), dma((2,)),
            dma((2, GROUPS)), dma((2, GROUPS)), dma((2,)), dma((2,)),
            dma((2, layers)), dma((layers, 2)),
        ],
        compiler_params=pltpu.CompilerParams(
            collective_id=0, has_side_effects=True, vmem_limit_bytes=32 * 1024 * 1024
        ),
    )(
        amplitudes.reshape(rows, width_k),
        tile_mask.reshape(rows, blocks),
        owners.reshape(rows, 1),
        col_panels.reshape(tw, nw),
        row_panels.reshape(tw, nw),
    )
    return result.reshape(1, 1, rows, cw)


def solution(mesh):
    small = mesh.shape["row"] == 2 and mesh.shape["col"] == 4
    return jax.shard_map(
        crossed if small else routed,
        mesh=mesh,
        in_specs=(
            P("row", "col", None, "layer"),
            P("row", "col", None, "layer"),
            P("row", "col", None, None),
            P("row", "col", "layer", None, None),
            P("row", "col", "layer", None, None),
        ),
        out_specs=P("row", "col", None, "layer"),
        check_vma=False,
    )
```

```python
import functools

import jax
import jax.numpy as jnp
from jax import lax
from jax.experimental import pallas as pl
from jax.experimental.pallas import tpu as pltpu
from jax.sharding import PartitionSpec as P

MESH = pl.DeviceIdType.MESH
GROUPS = 4


def from_behind(x, axis, by):
    length = lax.axis_size(axis)
    return lax.ppermute(x, axis, [(i, (i + by) % length) for i in range(length)])


def routed(amplitudes, tile_mask, owners, col_panels, row_panels):
    rows_here = amplitudes.shape[2]
    width_k = amplitudes.shape[3]
    blocks = tile_mask.shape[3]
    tile_width = width_k // blocks
    half_blocks = blocks // 2
    grid_rows = lax.axis_size("row")
    grid_cols = lax.axis_size("col")
    peer_count = grid_rows * grid_cols
    capacity = max(2, 2 * rows_here // peer_count)
    slot_count = peer_count * capacity
    keep_mask = tile_mask[0, 0].astype(jnp.bfloat16)
    masked = (
        amplitudes[0, 0].reshape(rows_here, blocks, tile_width) * keep_mask[:, :, None]
    ).reshape(rows_here, width_k)
    destined = owners[0, 0, :, 0]
    ids = jnp.arange(rows_here, dtype=jnp.int32)
    earlier = (destined[:, None] == destined[None, :]) & (ids[None, :] < ids[:, None])
    slot_rank = jnp.sum(earlier.astype(jnp.int32), axis=1)
    slot_index = destined * capacity + slot_rank
    source_of = jnp.zeros((slot_count,), jnp.int32).at[slot_index].set(ids)
    filled = jnp.zeros((slot_count,), jnp.int32).at[slot_index].set(1)
    outgoing = jnp.take(masked, source_of, axis=0) * filled[:, None].astype(jnp.bfloat16)
    arrived = lax.all_to_all(
        outgoing.reshape(peer_count, capacity, width_k),
        ("row", "col"),
        split_axis=0,
        concat_axis=0,
        tiled=True,
    )
    arrived = arrived.reshape(slot_count, width_k)
    col_panel = col_panels[0, 0, 0]
    row_panel = row_panels[0, 0, 0]
    partial_value = jnp.zeros((slot_count, col_panel.shape[1]), jnp.float32)
    for position in range(half_blocks):
        if position > 0:
            col_panel = from_behind(col_panel, "col", -1)
            row_panel = from_behind(row_panel, "row", -1)
        col_block = arrived[:, position * tile_width : (position + 1) * tile_width]
        row_block = arrived[
            :, (half_blocks + position) * tile_width : (half_blocks + position + 1) * tile_width
        ]
        partial_value = partial_value + jnp.dot(
            col_block, col_panel, preferred_element_type=jnp.float32
        )
        partial_value = partial_value + jnp.dot(
            row_block, row_panel, preferred_element_type=jnp.float32
        )
    rounded = partial_value.astype(jnp.bfloat16)
    returned = lax.all_to_all(
        rounded.reshape(peer_count, capacity, rounded.shape[1]),
        ("row", "col"),
        split_axis=0,
        concat_axis=0,
        tiled=True,
    )
    own_rows = jnp.take(returned.reshape(slot_count, rounded.shape[1]), slot_index, axis=0)
    result = lax.psum_scatter(
        own_rows.astype(jnp.float32).astype(jnp.bfloat16), "layer", scatter_dimension=1, tiled=True
    )
    return result.reshape(1, 1, rows_here, result.shape[1])


def kernel(layers, amp_hbm, mask_hbm, own_hbm, col_hbm, row_hbm, out, amp, mask, own, colp, rowp,
           panels, lhs, xs, xr, codes, codes_in, outb, inbox, load, ysend, yrecv, ssend, srecv, fsend, frecv, xsend, xrecv, osend, irecv):
    rows, tw, nw = amp.shape[0], colp.shape[0], colp.shape[1]
    gw, cw = nw // GROUPS, nw // layers
    x, q, z = lax.axis_index("row"), lax.axis_index("col"), lax.axis_index("layer")
    core = lax.rem(q, 2)
    sib, yq = q + 1 - 2 * core, lax.rem(q + 2, 4)
    ysib = yq + 1 - 2 * core
    cols = [q, sib, yq, ysib]
    other = 1 - x

    barrier = pltpu.get_barrier_semaphore()

    def greet(device):
        pl.semaphore_signal(barrier, inc=1, device_id=device, device_id_type=MESH)

    greet((x, yq, z))
    greet((x, sib, z))
    for n in range(layers):
        greet((other, q, n))

        @pl.when(n != z)
        def _():
            greet((x, q, n))

    def copy(src, dst, s, r, device):
        return pltpu.make_async_remote_copy(
            src_ref=src, dst_ref=dst, send_sem=s, recv_sem=r, device_id=device, device_id_type=MESH
        )

    def group(g):
        return pl.ds(g * gw, gw)

    loads = [pltpu.make_async_copy(a, b, load.at[i]) for i, (a, b) in enumerate(
        [(own_hbm, own), (mask_hbm, mask), (amp_hbm, amp), (col_hbm, colp), (row_hbm, rowp)])]
    for c in loads:
        c.start()

    own_panels = [col_hbm, row_hbm]
    to_y = [[copy(own_panels[k].at[:, group(g)], panels.at[k, 1, :, group(g)], ysend.at[k, g],
                  yrecv.at[k, g], (x, yq, z)) for k in range(2)] for g in range(GROUPS)]
    to_sib = [copy(own_panels[k], panels.at[k, 0], ssend.at[k], srecv.at[k], (x, sib, z))
              for k in range(2)]
    onward = [[copy(panels.at[k, 1, :, group(g)], panels.at[k, 2, :, group(g)], fsend.at[k, g],
                    frecv.at[k, g], (x, sib, z)) for k in range(2)] for g in range(GROUPS)]
    to_x = [
        copy(codes, codes_in, xsend.at[2], xrecv.at[2], (other, q, z)),
        copy(xs.at[:, pl.ds(0, tw)], xr, xsend.at[0], xrecv.at[0], (other, q, z)),
        copy(xs.at[:, pl.ds(tw, 4 * tw)], lhs.at[pl.ds(rows, rows), pl.ds(0, 4 * tw)],
             xsend.at[1], xrecv.at[1], (other, q, z)),
    ]

    def wide(a):
        return jnp.concatenate([a] * (tw // 128), axis=1)

    def flag(cond):
        return wide(cond.astype(jnp.float32).astype(jnp.bfloat16))

    def down(row):
        return jnp.transpose(jnp.broadcast_to(row.astype(jnp.float32), (128, rows)))

    pl.semaphore_wait(barrier, 2 * layers + 1)
    for c in to_y[0] + to_sib:
        c.start()
    for g in range(1, GROUPS):
        for c in to_y[g]:
            c.start()

    for c in loads[:3]:
        c.wait()
    dest = down(own[...]).astype(jnp.int32)
    dest_row = jnp.where(dest >= 4, 1, 0)
    dest_col = dest - 4 * dest_row
    here, there = flag(dest_row == x), flag(dest_row != x)

    def block(m):
        return amp[:, m * tw : (m + 1) * tw] * wide(down(mask[m : m + 1]).astype(jnp.bfloat16))

    codes[...] = jnp.broadcast_to(own[...] - 4 * jnp.where(own[...] >= 4, 1, 0), codes.shape).astype(
        jnp.float32
    ).astype(jnp.bfloat16)
    f32 = jnp.float32
    even = (block(4).astype(f32) + block(6).astype(f32)).astype(jnp.bfloat16)
    odd = (block(5).astype(f32) + block(7).astype(f32)).astype(jnp.bfloat16)
    own_row = even * here + odd * there
    xs[:, :tw] = odd * here + even * there
    to_x[0].start()
    to_x[1].start()
    col_blocks = [block(s) for s in range(4)]
    for j in range(4):
        met = sum(col_blocks[s] * flag(dest_col == lax.rem(cols[j] + 4 - s, 4)) for s in range(4))
        lhs[:rows, j * tw : (j + 1) * tw] = met * here
        xs[:, (1 + j) * tw : (2 + j) * tw] = met * there

    to_x[2].start()

    for j in range(4):
        meets = flag(dest_col == cols[j])
        lhs[:rows, (4 + j) * tw : (5 + j) * tw] = own_row * meets

    for c in loads[3:]:
        c.wait()
    for c in to_sib:
        c.wait_recv()
    for c in to_x:
        c.wait_recv()
    code = down(codes_in[...][:1])
    for j in range(4):
        meets = flag(code == cols[j].astype(jnp.float32))
        lhs[rows:, (4 + j) * tw : (5 + j) * tw] = xr[...] * meets

    def result(n, side):
        return copy(outb.at[side, n], inbox.at[z, side], osend.at[side, n], irecv.at[z, side],
                    (x if side == 0 else other, q, n))

    for g in range(GROUPS):
        for k in range(2):
            to_y[g][k].wait_recv()
            onward[g][k].start()
        total = jnp.zeros((2 * rows, gw), jnp.float32)
        for j in range(4):
            if j == 3:
                for k in range(2):
                    onward[g][k].wait_recv()
            col = colp[:, g * gw : (g + 1) * gw] if j == 0 else panels[0, j - 1, :, g * gw : (g + 1) * gw]
            row = rowp[:, g * gw : (g + 1) * gw] if j == 0 else panels[1, j - 1, :, g * gw : (g + 1) * gw]
            total += jnp.dot(lhs[:, j * tw : (j + 1) * tw], col, preferred_element_type=jnp.float32)
            total += jnp.dot(
                lhs[:, (4 + j) * tw : (5 + j) * tw], row, preferred_element_type=jnp.float32
            )
        total = total.astype(jnp.bfloat16)
        for i in range(layers // GROUPS):
            n = g * (layers // GROUPS) + i
            outb[0, n] = total[:rows, i * cw : (i + 1) * cw]
            outb[1, n] = total[rows:, i * cw : (i + 1) * cw]
            result(n, 1).start()

            @pl.when(n != z)
            def _():
                result(n, 0).start()

            @pl.when(n == z)
            def _():
                inbox[n, 0] = outb[0, n]

    def arrived(n, side):
        copy(outb.at[side, n], inbox.at[n, side], osend.at[side, n], irecv.at[n, side],
             (x if side == 0 else other, q, n)).wait_recv()

    for n in range(layers):
        arrived(n, 1)

        @pl.when(n != z)
        def _():
            arrived(n, 0)

    result_sum = jnp.zeros((rows, cw), jnp.float32)
    for n in range(layers):
        result_sum += inbox[n, 0].astype(jnp.float32) + inbox[n, 1].astype(jnp.float32)
    out[...] = result_sum.astype(out.dtype)

    for c in to_sib + to_x:
        c.wait_send()
    for g in range(GROUPS):
        for c in to_y[g] + onward[g]:
            c.wait_send()
    for n in range(layers):
        result(n, 1).wait_send()

        @pl.when(n != z)
        def _():
            result(n, 0).wait_send()


def crossed(amplitudes, tile_mask, owners, col_panels, row_panels):
    layers = lax.axis_size("layer")
    rows, width_k = amplitudes.shape[2:]
    tw, nw = col_panels.shape[3:]
    blocks = tile_mask.shape[3]
    cw = nw // layers
    dma = pltpu.SemaphoreType.DMA
    bf16 = jnp.bfloat16
    vmem = pl.BlockSpec(memory_space=pltpu.VMEM)
    result = pl.pallas_call(
        functools.partial(kernel, layers),
        out_shape=jax.ShapeDtypeStruct((rows, cw), bf16),
        in_specs=[pl.BlockSpec(memory_space=pltpu.HBM)] * 5,
        out_specs=vmem,
        scratch_shapes=[
            pltpu.VMEM((rows, width_k), bf16),
            pltpu.VMEM((blocks, rows), jnp.int32),
            pltpu.VMEM((1, rows), jnp.int32),
            pltpu.VMEM((tw, nw), bf16),
            pltpu.VMEM((tw, nw), bf16),
            pltpu.VMEM((2, 3, tw, nw), bf16),
            pltpu.VMEM((2 * rows, 8 * tw), bf16),
            pltpu.VMEM((rows, 5 * tw), bf16),
            pltpu.VMEM((rows, tw), bf16),
            pltpu.VMEM((16, rows), bf16),
            pltpu.VMEM((16, rows), bf16),
            pltpu.VMEM((2, layers, rows, cw), bf16),
            pltpu.VMEM((layers, 2, rows, cw), bf16),
            dma((5,)), dma((2, GROUPS)), dma((2, GROUPS)), dma((2,)), dma((2,)),
            dma((2, GROUPS)), dma((2, GROUPS)), dma((3,)), dma((3,)),
            dma((2, layers)), dma((layers, 2)),
        ],
        compiler_params=pltpu.CompilerParams(
            collective_id=0, has_side_effects=True, vmem_limit_bytes=60 * 1024 * 1024
        ),
    )(
        amplitudes.reshape(rows, width_k),
        tile_mask.reshape(rows, blocks).T,
        owners.reshape(1, rows),
        col_panels.reshape(tw, nw),
        row_panels.reshape(tw, nw),
    )
    return result.reshape(1, 1, rows, cw)


def solution(mesh):
    small = mesh.shape["row"] == 2 and mesh.shape["col"] == 4
    return jax.shard_map(
        crossed if small else routed,
        mesh=mesh,
        in_specs=(
            P("row", "col", None, "layer"),
            P("row", "col", None, "layer"),
            P("row", "col", None, None),
            P("row", "col", "layer", None, None),
            P("row", "col", "layer", None, None),
        ),
        out_specs=P("row", "col", None, "layer"),
        check_vma=False,
    )
```

```python
import functools

import jax
import jax.numpy as jnp
from jax import lax
from jax.experimental import pallas as pl
from jax.experimental.pallas import tpu as pltpu
from jax.sharding import PartitionSpec as P

MESH = pl.DeviceIdType.MESH


def from_behind(x, axis, by):
    length = lax.axis_size(axis)
    return lax.ppermute(x, axis, [(i, (i + by) % length) for i in range(length)])


def routed(amplitudes, tile_mask, owners, col_panels, row_panels):
    rows_here = amplitudes.shape[2]
    width_k = amplitudes.shape[3]
    blocks = tile_mask.shape[3]
    tile_width = width_k // blocks
    half_blocks = blocks // 2
    grid_rows = lax.axis_size("row")
    grid_cols = lax.axis_size("col")
    peer_count = grid_rows * grid_cols
    capacity = max(2, 2 * rows_here // peer_count)
    slot_count = peer_count * capacity
    keep_mask = tile_mask[0, 0].astype(jnp.bfloat16)
    masked = (
        amplitudes[0, 0].reshape(rows_here, blocks, tile_width) * keep_mask[:, :, None]
    ).reshape(rows_here, width_k)
    destined = owners[0, 0, :, 0]
    ids = jnp.arange(rows_here, dtype=jnp.int32)
    earlier = (destined[:, None] == destined[None, :]) & (ids[None, :] < ids[:, None])
    slot_rank = jnp.sum(earlier.astype(jnp.int32), axis=1)
    slot_index = destined * capacity + slot_rank
    source_of = jnp.zeros((slot_count,), jnp.int32).at[slot_index].set(ids)
    filled = jnp.zeros((slot_count,), jnp.int32).at[slot_index].set(1)
    outgoing = jnp.take(masked, source_of, axis=0) * filled[:, None].astype(jnp.bfloat16)
    arrived = lax.all_to_all(
        outgoing.reshape(peer_count, capacity, width_k),
        ("row", "col"),
        split_axis=0,
        concat_axis=0,
        tiled=True,
    )
    arrived = arrived.reshape(slot_count, width_k)
    col_panel = col_panels[0, 0, 0]
    row_panel = row_panels[0, 0, 0]
    partial_value = jnp.zeros((slot_count, col_panel.shape[1]), jnp.float32)
    for position in range(half_blocks):
        if position > 0:
            col_panel = from_behind(col_panel, "col", -1)
            row_panel = from_behind(row_panel, "row", -1)
        col_block = arrived[:, position * tile_width : (position + 1) * tile_width]
        row_block = arrived[
            :, (half_blocks + position) * tile_width : (half_blocks + position + 1) * tile_width
        ]
        partial_value = partial_value + jnp.dot(
            col_block, col_panel, preferred_element_type=jnp.float32
        )
        partial_value = partial_value + jnp.dot(
            row_block, row_panel, preferred_element_type=jnp.float32
        )
    rounded = partial_value.astype(jnp.bfloat16)
    returned = lax.all_to_all(
        rounded.reshape(peer_count, capacity, rounded.shape[1]),
        ("row", "col"),
        split_axis=0,
        concat_axis=0,
        tiled=True,
    )
    own_rows = jnp.take(returned.reshape(slot_count, rounded.shape[1]), slot_index, axis=0)
    result = lax.psum_scatter(
        own_rows.astype(jnp.float32).astype(jnp.bfloat16), "layer", scatter_dimension=1, tiled=True
    )
    return result.reshape(1, 1, rows_here, result.shape[1])


def kernel(layers, amp_hbm, mask_hbm, own_hbm, col_hbm, row_hbm, out, amp, mask, own, colp, rowp,
           panels, lhs, xs, xr, codes, codes_in, outb, inbox, answer, ready, load, ysend, yrecv, ssend, srecv, fsend, frecv, xsend, xrecv, osend, irecv):
    rows, tw, nw = amp.shape[0], colp.shape[0], colp.shape[1]
    cw = nw // layers
    x, q, z = lax.axis_index("row"), lax.axis_index("col"), lax.axis_index("layer")
    core = lax.rem(q, 2)
    sib, yq = q + 1 - 2 * core, lax.rem(q + 2, 4)
    ysib = yq + 1 - 2 * core
    cols = [q, sib, yq, ysib]
    other = 1 - x

    loads = [pltpu.make_async_copy(a, b, load.at[i]) for i, (a, b) in enumerate(
        [(own_hbm, own), (mask_hbm, mask), (amp_hbm, amp), (col_hbm, colp), (row_hbm, rowp)])]
    for c in loads:
        c.start()

    barrier = pltpu.get_barrier_semaphore()

    def greet(device):
        pl.semaphore_signal(barrier, inc=1, device_id=device, device_id_type=MESH)

    odd = lax.rem(x + q // 2 + core, 2) == 1
    near = [(x, yq, z), (x, sib, z), (other, q, z)]

    @pl.when(odd)
    def _():
        for device in near:
            greet(device)

    @pl.when(jnp.logical_not(odd))
    def _():
        pl.semaphore_wait(barrier, len(near))
        for device in near:
            pl.semaphore_signal(answer, inc=1, device_id=device, device_id_type=MESH)

    def copy(src, dst, s, r, device):
        return pltpu.make_async_remote_copy(
            src_ref=src, dst_ref=dst, send_sem=s, recv_sem=r, device_id=device, device_id_type=MESH
        )

    hops = [k for k in range(1, layers)]
    hops = sorted(hops, key=lambda k: (k != layers // 2, k)) + [0]
    keepers = [lax.rem(z + k, layers) for k in hops]

    def group(g):
        return pl.ds(pl.multiple_of(keepers[g] * cw, cw), cw)

    own_panels = [col_hbm, row_hbm]
    to_y = [[copy(own_panels[k].at[:, group(g)], panels.at[k, 1, :, group(g)], ysend.at[k, g],
                  yrecv.at[k, g], (x, yq, z)) for k in range(2)] for g in range(layers)]
    to_sib = [copy(own_panels[k], panels.at[k, 0], ssend.at[k], srecv.at[k], (x, sib, z))
              for k in range(2)]
    onward = [[copy(panels.at[k, 1, :, group(g)], panels.at[k, 2, :, group(g)], fsend.at[k, g],
                    frecv.at[k, g], (x, sib, z)) for k in range(2)] for g in range(layers)]
    to_x = [
        copy(codes, codes_in, xsend.at[2], xrecv.at[2], (other, q, z)),
        copy(xs.at[:, pl.ds(0, tw)], xr, xsend.at[0], xrecv.at[0], (other, q, z)),
        copy(xs.at[:, pl.ds(tw, 4 * tw)], lhs.at[pl.ds(rows, rows), pl.ds(0, 4 * tw)],
             xsend.at[1], xrecv.at[1], (other, q, z)),
    ]

    def wide(a):
        return jnp.concatenate([a] * (tw // 128), axis=1)

    def flag(cond):
        return wide(cond.astype(jnp.float32).astype(jnp.bfloat16))

    def down(row):
        return jnp.transpose(jnp.broadcast_to(row.astype(jnp.float32), (128, rows)))

    @pl.when(odd)
    def _():
        pl.semaphore_wait(answer, len(near))

    for c in to_y[0] + to_sib:
        c.start()
    for g in range(1, layers):
        for c in to_y[g]:
            c.start()

    @pl.when(odd)
    def _():
        for n in range(layers):

            @pl.when(n != z)
            def _():
                greet((x, q, n))

    for c in loads[:3]:
        c.wait()
    dest = down(own[...]).astype(jnp.int32)
    dest_row = jnp.where(dest >= 4, 1, 0)
    dest_col = dest - 4 * dest_row
    here, there = flag(dest_row == x), flag(dest_row != x)

    def block(m):
        return amp[:, m * tw : (m + 1) * tw] * wide(down(mask[m : m + 1]).astype(jnp.bfloat16))

    codes[...] = jnp.broadcast_to(own[...] - 4 * jnp.where(own[...] >= 4, 1, 0), codes.shape).astype(
        jnp.float32
    ).astype(jnp.bfloat16)
    f32 = jnp.float32
    evens = (block(4).astype(f32) + block(6).astype(f32)).astype(jnp.bfloat16)
    odds = (block(5).astype(f32) + block(7).astype(f32)).astype(jnp.bfloat16)
    own_row = evens * here + odds * there
    xs[:, :tw] = odds * here + evens * there
    to_x[0].start()
    to_x[1].start()
    col_blocks = [block(s) for s in range(4)]
    for j in range(4):
        met = sum(col_blocks[s] * flag(dest_col == lax.rem(cols[j] + 4 - s, 4)) for s in range(4))
        lhs[:rows, j * tw : (j + 1) * tw] = met * here
        xs[:, (1 + j) * tw : (2 + j) * tw] = met * there

    to_x[2].start()

    for j in range(4):
        meets = flag(dest_col == cols[j])
        lhs[:rows, (4 + j) * tw : (5 + j) * tw] = own_row * meets

    for c in loads[3:]:
        c.wait()
    for c in to_sib:
        c.wait_recv()
    for c in to_x:
        c.wait_recv()
    code = down(codes_in[...][:1])
    for j in range(4):
        meets = flag(code == cols[j].astype(jnp.float32))
        lhs[rows:, (4 + j) * tw : (5 + j) * tw] = xr[...] * meets

    @pl.when(odd)
    def _():
        pl.semaphore_wait(barrier, layers - 1)
        pl.semaphore_signal(ready, inc=1, device_id=(other, q, z), device_id_type=MESH)

    @pl.when(jnp.logical_not(odd))
    def _():
        pl.semaphore_wait(ready, 1)

    def result(g, side):
        return copy(outb.at[side, g], inbox.at[side, g], osend.at[side, g], irecv.at[side, g],
                    (x if side == 0 else other, q, keepers[g]))

    for g in range(layers):
        for k in range(2):
            to_y[g][k].wait_recv()
            onward[g][k].start()
        total = jnp.zeros((2 * rows, cw), jnp.float32)
        for j in range(4):
            if j == 3:
                for k in range(2):
                    onward[g][k].wait_recv()
            col = colp[:, group(g)] if j == 0 else panels[0, j - 1, :, group(g)]
            row = rowp[:, group(g)] if j == 0 else panels[1, j - 1, :, group(g)]
            total += jnp.dot(lhs[:, j * tw : (j + 1) * tw], col, preferred_element_type=jnp.float32)
            total += jnp.dot(
                lhs[:, (4 + j) * tw : (5 + j) * tw], row, preferred_element_type=jnp.float32
            )
        outb[1, g] = total[rows:].astype(jnp.bfloat16)
        result(g, 1).start()
        outb[0, g] = total[:rows].astype(jnp.bfloat16)
        if g < layers - 1:
            result(g, 0).start()

    kept = outb[0, layers - 1].astype(jnp.float32)
    for g in range(layers):
        if g < layers - 1:
            result(g, 0).wait_recv()
            kept += inbox[0, g].astype(jnp.float32)
        result(g, 1).wait_recv()
        kept += inbox[1, g].astype(jnp.float32)
    out[...] = kept.astype(out.dtype)

    for c in to_sib + to_x:
        c.wait_send()
    for g in range(layers):
        for c in to_y[g] + onward[g]:
            c.wait_send()
    for g in range(layers):
        result(g, 1).wait_send()
        if g < layers - 1:
            result(g, 0).wait_send()


def crossed(amplitudes, tile_mask, owners, col_panels, row_panels):
    layers = lax.axis_size("layer")
    rows, width_k = amplitudes.shape[2:]
    tw, nw = col_panels.shape[3:]
    blocks = tile_mask.shape[3]
    cw = nw // layers
    dma = pltpu.SemaphoreType.DMA
    bf16 = jnp.bfloat16
    vmem = pl.BlockSpec(memory_space=pltpu.VMEM)
    result = pl.pallas_call(
        functools.partial(kernel, layers),
        out_shape=jax.ShapeDtypeStruct((rows, cw), bf16),
        in_specs=[pl.BlockSpec(memory_space=pltpu.HBM)] * 5,
        out_specs=vmem,
        scratch_shapes=[
            pltpu.VMEM((rows, width_k), bf16),
            pltpu.VMEM((blocks, rows), jnp.int32),
            pltpu.VMEM((1, rows), jnp.int32),
            pltpu.VMEM((tw, nw), bf16),
            pltpu.VMEM((tw, nw), bf16),
            pltpu.VMEM((2, 3, tw, nw), bf16),
            pltpu.VMEM((2 * rows, 8 * tw), bf16),
            pltpu.VMEM((rows, 5 * tw), bf16),
            pltpu.VMEM((rows, tw), bf16),
            pltpu.VMEM((16, rows), bf16),
            pltpu.VMEM((16, rows), bf16),
            pltpu.VMEM((2, layers, rows, cw), bf16),
            pltpu.VMEM((2, layers, rows, cw), bf16),
            pltpu.SemaphoreType.REGULAR, pltpu.SemaphoreType.REGULAR,
            dma((5,)), dma((2, layers)), dma((2, layers)), dma((2,)), dma((2,)),
            dma((2, layers)), dma((2, layers)), dma((3,)), dma((3,)),
            dma((2, layers)), dma((2, layers)),
        ],
        compiler_params=pltpu.CompilerParams(
            collective_id=0, has_side_effects=True, vmem_limit_bytes=60 * 1024 * 1024
        ),
    )(
        amplitudes.reshape(rows, width_k),
        tile_mask.reshape(rows, blocks).T,
        owners.reshape(1, rows),
        col_panels.reshape(tw, nw),
        row_panels.reshape(tw, nw),
    )
    return result.reshape(1, 1, rows, cw)


def solution(mesh):
    small = mesh.shape["row"] == 2 and mesh.shape["col"] == 4
    return jax.shard_map(
        crossed if small else routed,
        mesh=mesh,
        in_specs=(
            P("row", "col", None, "layer"),
            P("row", "col", None, "layer"),
            P("row", "col", None, None),
            P("row", "col", "layer", None, None),
            P("row", "col", "layer", None, None),
        ),
        out_specs=P("row", "col", None, "layer"),
        check_vma=False,
    )
```

```python
import functools

import jax
import jax.numpy as jnp
from jax import lax
from jax.experimental import pallas as pl
from jax.experimental.pallas import tpu as pltpu
from jax.sharding import PartitionSpec as P

MESH = pl.DeviceIdType.MESH


def from_behind(x, axis, by):
    length = lax.axis_size(axis)
    return lax.ppermute(x, axis, [(i, (i + by) % length) for i in range(length)])


def routed(amplitudes, tile_mask, owners, col_panels, row_panels):
    rows_here = amplitudes.shape[2]
    width_k = amplitudes.shape[3]
    blocks = tile_mask.shape[3]
    tile_width = width_k // blocks
    half_blocks = blocks // 2
    grid_rows = lax.axis_size("row")
    grid_cols = lax.axis_size("col")
    peer_count = grid_rows * grid_cols
    capacity = max(2, 2 * rows_here // peer_count)
    slot_count = peer_count * capacity
    keep_mask = tile_mask[0, 0].astype(jnp.bfloat16)
    masked = (
        amplitudes[0, 0].reshape(rows_here, blocks, tile_width) * keep_mask[:, :, None]
    ).reshape(rows_here, width_k)
    destined = owners[0, 0, :, 0]
    ids = jnp.arange(rows_here, dtype=jnp.int32)
    earlier = (destined[:, None] == destined[None, :]) & (ids[None, :] < ids[:, None])
    slot_rank = jnp.sum(earlier.astype(jnp.int32), axis=1)
    slot_index = destined * capacity + slot_rank
    source_of = jnp.zeros((slot_count,), jnp.int32).at[slot_index].set(ids)
    filled = jnp.zeros((slot_count,), jnp.int32).at[slot_index].set(1)
    outgoing = jnp.take(masked, source_of, axis=0) * filled[:, None].astype(jnp.bfloat16)
    arrived = lax.all_to_all(
        outgoing.reshape(peer_count, capacity, width_k),
        ("row", "col"),
        split_axis=0,
        concat_axis=0,
        tiled=True,
    )
    arrived = arrived.reshape(slot_count, width_k)
    col_panel = col_panels[0, 0, 0]
    row_panel = row_panels[0, 0, 0]
    partial_value = jnp.zeros((slot_count, col_panel.shape[1]), jnp.float32)
    for position in range(half_blocks):
        if position > 0:
            col_panel = from_behind(col_panel, "col", -1)
            row_panel = from_behind(row_panel, "row", -1)
        col_block = arrived[:, position * tile_width : (position + 1) * tile_width]
        row_block = arrived[
            :, (half_blocks + position) * tile_width : (half_blocks + position + 1) * tile_width
        ]
        partial_value = partial_value + jnp.dot(
            col_block, col_panel, preferred_element_type=jnp.float32
        )
        partial_value = partial_value + jnp.dot(
            row_block, row_panel, preferred_element_type=jnp.float32
        )
    rounded = partial_value.astype(jnp.bfloat16)
    returned = lax.all_to_all(
        rounded.reshape(peer_count, capacity, rounded.shape[1]),
        ("row", "col"),
        split_axis=0,
        concat_axis=0,
        tiled=True,
    )
    own_rows = jnp.take(returned.reshape(slot_count, rounded.shape[1]), slot_index, axis=0)
    result = lax.psum_scatter(
        own_rows.astype(jnp.float32).astype(jnp.bfloat16), "layer", scatter_dimension=1, tiled=True
    )
    return result.reshape(1, 1, rows_here, result.shape[1])


def kernel(layers, amp_hbm, mask_hbm, own_hbm, col_hbm, row_hbm, out, amp, mask, own, colp, rowp,
           panels, lhs, xs, xr, codes, codes_in, outb, inbox, answer, ready, load, ysend, yrecv, ssend, srecv, fsend, frecv, xsend, xrecv, osend, irecv):
    rows, tw, nw = amp.shape[0], colp.shape[0], colp.shape[1]
    cw = nw // layers
    x, q, z = lax.axis_index("row"), lax.axis_index("col"), lax.axis_index("layer")
    core = lax.rem(q, 2)
    sib, yq = q + 1 - 2 * core, lax.rem(q + 2, 4)
    ysib = yq + 1 - 2 * core
    cols = [q, sib, yq, ysib]
    other = 1 - x

    loads = [pltpu.make_async_copy(a, b, load.at[i]) for i, (a, b) in enumerate(
        [(own_hbm, own), (mask_hbm, mask), (amp_hbm, amp), (col_hbm, colp), (row_hbm, rowp)])]
    for c in loads:
        c.start()

    barrier = pltpu.get_barrier_semaphore()

    def greet(device):
        pl.semaphore_signal(barrier, inc=1, device_id=device, device_id_type=MESH)

    odd = lax.rem(x + q // 2 + core, 2) == 1
    near = [(x, yq, z), (x, sib, z), (other, q, z)]

    @pl.when(odd)
    def _():
        for device in near:
            greet(device)

    @pl.when(jnp.logical_not(odd))
    def _():
        pl.semaphore_wait(barrier, len(near))
        for device in near:
            pl.semaphore_signal(answer, inc=1, device_id=device, device_id_type=MESH)

    def copy(src, dst, s, r, device):
        return pltpu.make_async_remote_copy(
            src_ref=src, dst_ref=dst, send_sem=s, recv_sem=r, device_id=device, device_id_type=MESH
        )

    hops = [k for k in range(1, layers)]
    hops = sorted(hops, key=lambda k: (k != layers // 2, k)) + [0]
    keepers = [lax.rem(z + k, layers) for k in hops]

    def group(g):
        return pl.ds(pl.multiple_of(keepers[g] * cw, cw), cw)

    own_panels = [col_hbm, row_hbm]
    to_y = [[copy(own_panels[k].at[:, group(g)], panels.at[k, 1, :, group(g)], ysend.at[k, g],
                  yrecv.at[k, g], (x, yq, z)) for k in range(2)] for g in range(layers)]
    to_sib = [copy(own_panels[k], panels.at[k, 0], ssend.at[k], srecv.at[k], (x, sib, z))
              for k in range(2)]
    onward = [[copy(panels.at[k, 1, :, group(g)], panels.at[k, 2, :, group(g)], fsend.at[k, g],
                    frecv.at[k, g], (x, sib, z)) for k in range(2)] for g in range(layers)]
    to_x = [
        copy(codes, codes_in, xsend.at[2], xrecv.at[2], (other, q, z)),
        copy(xs.at[:, pl.ds(0, tw)], xr, xsend.at[0], xrecv.at[0], (other, q, z)),
        copy(xs.at[:, pl.ds(tw, 4 * tw)], lhs.at[pl.ds(rows, rows), pl.ds(0, 4 * tw)],
             xsend.at[1], xrecv.at[1], (other, q, z)),
    ]

    def wide(a):
        return jnp.concatenate([a] * (tw // 128), axis=1)

    def flag(cond):
        return wide(cond.astype(jnp.float32).astype(jnp.bfloat16))

    def down(row):
        return jnp.transpose(jnp.broadcast_to(row.astype(jnp.float32), (128, rows)))

    @pl.when(odd)
    def _():
        pl.semaphore_wait(answer, len(near))

    for c in to_y[0] + to_sib:
        c.start()
    for g in range(1, layers):
        for c in to_y[g]:
            c.start()

    @pl.when(odd)
    def _():
        for n in range(layers):

            @pl.when(n != z)
            def _():
                greet((x, q, n))

    for c in loads[:3]:
        c.wait()
    dest = down(own[...]).astype(jnp.int32)
    dest_row = jnp.where(dest >= 4, 1, 0)
    dest_col = dest - 4 * dest_row
    here, there = flag(dest_row == x), flag(dest_row != x)

    def block(m):
        return amp[:, m * tw : (m + 1) * tw] * wide(down(mask[m : m + 1]).astype(jnp.bfloat16))

    codes[...] = jnp.broadcast_to(own[...] - 4 * jnp.where(own[...] >= 4, 1, 0), codes.shape).astype(
        jnp.float32
    ).astype(jnp.bfloat16)
    f32 = jnp.float32
    evens = (block(4).astype(f32) + block(6).astype(f32)).astype(jnp.bfloat16)
    odds = (block(5).astype(f32) + block(7).astype(f32)).astype(jnp.bfloat16)
    own_row = evens * here + odds * there
    xs[:, :tw] = odds * here + evens * there
    to_x[0].start()
    to_x[1].start()
    col_blocks = [block(s) for s in range(4)]
    for j in range(4):
        met = sum(col_blocks[s] * flag(dest_col == lax.rem(cols[j] + 4 - s, 4)) for s in range(4))
        lhs[:rows, j * tw : (j + 1) * tw] = met * here
        xs[:, (1 + j) * tw : (2 + j) * tw] = met * there

    to_x[2].start()

    for j in range(4):
        meets = flag(dest_col == cols[j])
        lhs[:rows, (4 + j) * tw : (5 + j) * tw] = own_row * meets

    def pass_on(g):
        for k in range(2):
            to_y[g][k].wait_recv()
            onward[g][k].start()

    for c in loads[3:]:
        c.wait()
    pass_on(0)
    for c in to_sib:
        c.wait_recv()
    for c in to_x:
        c.wait_recv()
    code = down(codes_in[...][:1])
    for j in range(4):
        meets = flag(code == cols[j].astype(jnp.float32))
        lhs[rows:, (4 + j) * tw : (5 + j) * tw] = xr[...] * meets

    @pl.when(odd)
    def _():
        pl.semaphore_wait(barrier, layers - 1)
        pl.semaphore_signal(ready, inc=1, device_id=(other, q, z), device_id_type=MESH)

    @pl.when(jnp.logical_not(odd))
    def _():
        pl.semaphore_wait(ready, 1)

    def result(g, side):
        return copy(outb.at[side, g], inbox.at[side, g], osend.at[side, g], irecv.at[side, g],
                    (x if side == 0 else other, q, keepers[g]))

    for g in range(layers):
        if g + 1 < layers:
            pass_on(g + 1)
        total = jnp.zeros((2 * rows, cw), jnp.float32)
        for j in range(4):
            if j == 3:
                for k in range(2):
                    onward[g][k].wait_recv()
            col = colp[:, group(g)] if j == 0 else panels[0, j - 1, :, group(g)]
            row = rowp[:, group(g)] if j == 0 else panels[1, j - 1, :, group(g)]
            total += jnp.dot(lhs[:, j * tw : (j + 1) * tw], col, preferred_element_type=jnp.float32)
            total += jnp.dot(
                lhs[:, (4 + j) * tw : (5 + j) * tw], row, preferred_element_type=jnp.float32
            )
        outb[1, g] = total[rows:].astype(jnp.bfloat16)
        result(g, 1).start()
        outb[0, g] = total[:rows].astype(jnp.bfloat16)
        if g < layers - 1:
            result(g, 0).start()

    kept = outb[0, layers - 1].astype(jnp.float32)
    for g in range(layers):
        if g < layers - 1:
            result(g, 0).wait_recv()
            kept += inbox[0, g].astype(jnp.float32)
        result(g, 1).wait_recv()
        kept += inbox[1, g].astype(jnp.float32)
    out[...] = kept.astype(out.dtype)

    for c in to_sib + to_x:
        c.wait_send()
    for g in range(layers):
        for c in to_y[g] + onward[g]:
            c.wait_send()
    for g in range(layers):
        result(g, 1).wait_send()
        if g < layers - 1:
            result(g, 0).wait_send()


def crossed(amplitudes, tile_mask, owners, col_panels, row_panels):
    layers = lax.axis_size("layer")
    rows, width_k = amplitudes.shape[2:]
    tw, nw = col_panels.shape[3:]
    blocks = tile_mask.shape[3]
    cw = nw // layers
    dma = pltpu.SemaphoreType.DMA
    bf16 = jnp.bfloat16
    vmem = pl.BlockSpec(memory_space=pltpu.VMEM)
    result = pl.pallas_call(
        functools.partial(kernel, layers),
        out_shape=jax.ShapeDtypeStruct((rows, cw), bf16),
        in_specs=[pl.BlockSpec(memory_space=pltpu.HBM)] * 5,
        out_specs=vmem,
        scratch_shapes=[
            pltpu.VMEM((rows, width_k), bf16),
            pltpu.VMEM((blocks, rows), jnp.int32),
            pltpu.VMEM((1, rows), jnp.int32),
            pltpu.VMEM((tw, nw), bf16),
            pltpu.VMEM((tw, nw), bf16),
            pltpu.VMEM((2, 3, tw, nw), bf16),
            pltpu.VMEM((2 * rows, 8 * tw), bf16),
            pltpu.VMEM((rows, 5 * tw), bf16),
            pltpu.VMEM((rows, tw), bf16),
            pltpu.VMEM((16, rows), bf16),
            pltpu.VMEM((16, rows), bf16),
            pltpu.VMEM((2, layers, rows, cw), bf16),
            pltpu.VMEM((2, layers, rows, cw), bf16),
            pltpu.SemaphoreType.REGULAR, pltpu.SemaphoreType.REGULAR,
            dma((5,)), dma((2, layers)), dma((2, layers)), dma((2,)), dma((2,)),
            dma((2, layers)), dma((2, layers)), dma((3,)), dma((3,)),
            dma((2, layers)), dma((2, layers)),
        ],
        compiler_params=pltpu.CompilerParams(
            collective_id=0, has_side_effects=True, vmem_limit_bytes=60 * 1024 * 1024
        ),
    )(
        amplitudes.reshape(rows, width_k),
        tile_mask.reshape(rows, blocks).T,
        owners.reshape(1, rows),
        col_panels.reshape(tw, nw),
        row_panels.reshape(tw, nw),
    )
    return result.reshape(1, 1, rows, cw)


def solution(mesh):
    small = mesh.shape["row"] == 2 and mesh.shape["col"] == 4
    return jax.shard_map(
        crossed if small else routed,
        mesh=mesh,
        in_specs=(
            P("row", "col", None, "layer"),
            P("row", "col", None, "layer"),
            P("row", "col", None, None),
            P("row", "col", "layer", None, None),
            P("row", "col", "layer", None, None),
        ),
        out_specs=P("row", "col", None, "layer"),
        check_vma=False,
    )
```

```python
import functools

import jax
import jax.numpy as jnp
from jax import lax
from jax.experimental import pallas as pl
from jax.experimental.pallas import tpu as pltpu
from jax.sharding import PartitionSpec as P

MESH = pl.DeviceIdType.MESH


def from_behind(x, axis, by):
    length = lax.axis_size(axis)
    return lax.ppermute(x, axis, [(i, (i + by) % length) for i in range(length)])


def routed(amplitudes, tile_mask, owners, col_panels, row_panels):
    rows_here = amplitudes.shape[2]
    width_k = amplitudes.shape[3]
    blocks = tile_mask.shape[3]
    tile_width = width_k // blocks
    half_blocks = blocks // 2
    grid_rows = lax.axis_size("row")
    grid_cols = lax.axis_size("col")
    peer_count = grid_rows * grid_cols
    capacity = max(2, 2 * rows_here // peer_count)
    slot_count = peer_count * capacity
    keep_mask = tile_mask[0, 0].astype(jnp.bfloat16)
    masked = (
        amplitudes[0, 0].reshape(rows_here, blocks, tile_width) * keep_mask[:, :, None]
    ).reshape(rows_here, width_k)
    destined = owners[0, 0, :, 0]
    ids = jnp.arange(rows_here, dtype=jnp.int32)
    earlier = (destined[:, None] == destined[None, :]) & (ids[None, :] < ids[:, None])
    slot_rank = jnp.sum(earlier.astype(jnp.int32), axis=1)
    slot_index = destined * capacity + slot_rank
    source_of = jnp.zeros((slot_count,), jnp.int32).at[slot_index].set(ids)
    filled = jnp.zeros((slot_count,), jnp.int32).at[slot_index].set(1)
    outgoing = jnp.take(masked, source_of, axis=0) * filled[:, None].astype(jnp.bfloat16)
    arrived = lax.all_to_all(
        outgoing.reshape(peer_count, capacity, width_k),
        ("row", "col"),
        split_axis=0,
        concat_axis=0,
        tiled=True,
    )
    arrived = arrived.reshape(slot_count, width_k)
    col_panel = col_panels[0, 0, 0]
    row_panel = row_panels[0, 0, 0]
    partial_value = jnp.zeros((slot_count, col_panel.shape[1]), jnp.float32)
    for position in range(half_blocks):
        if position > 0:
            col_panel = from_behind(col_panel, "col", -1)
            row_panel = from_behind(row_panel, "row", -1)
        col_block = arrived[:, position * tile_width : (position + 1) * tile_width]
        row_block = arrived[
            :, (half_blocks + position) * tile_width : (half_blocks + position + 1) * tile_width
        ]
        partial_value = partial_value + jnp.dot(
            col_block, col_panel, preferred_element_type=jnp.float32
        )
        partial_value = partial_value + jnp.dot(
            row_block, row_panel, preferred_element_type=jnp.float32
        )
    rounded = partial_value.astype(jnp.bfloat16)
    returned = lax.all_to_all(
        rounded.reshape(peer_count, capacity, rounded.shape[1]),
        ("row", "col"),
        split_axis=0,
        concat_axis=0,
        tiled=True,
    )
    own_rows = jnp.take(returned.reshape(slot_count, rounded.shape[1]), slot_index, axis=0)
    result = lax.psum_scatter(
        own_rows.astype(jnp.float32).astype(jnp.bfloat16), "layer", scatter_dimension=1, tiled=True
    )
    return result.reshape(1, 1, rows_here, result.shape[1])


def kernel(layers, amp_hbm, mask_hbm, own_hbm, col_hbm, row_hbm, out, amp, mask, own, colp, rowp,
           panels, lhs, xs, xr, codes, codes_in, outb, inbox, answer, ready, load, ysend, yrecv, ssend, srecv, fsend, frecv, xsend, xrecv, osend, irecv):
    rows, tw, nw = amp.shape[0], colp.shape[0], colp.shape[1]
    cw = nw // layers
    x, q, z = lax.axis_index("row"), lax.axis_index("col"), lax.axis_index("layer")
    core = lax.rem(q, 2)
    sib, yq = q + 1 - 2 * core, lax.rem(q + 2, 4)
    ysib = yq + 1 - 2 * core
    cols = [q, sib, yq, ysib]
    other = 1 - x

    loads = [pltpu.make_async_copy(a, b, load.at[i]) for i, (a, b) in enumerate(
        [(own_hbm, own), (mask_hbm, mask), (amp_hbm, amp), (col_hbm, colp), (row_hbm, rowp)])]
    for c in loads:
        c.start()

    barrier = pltpu.get_barrier_semaphore()

    def greet(device):
        pl.semaphore_signal(barrier, inc=1, device_id=device, device_id_type=MESH)

    odd = lax.rem(x + q // 2 + core, 2) == 1
    near = [(x, yq, z), (x, sib, z), (other, q, z)]

    @pl.when(odd)
    def _():
        for device in near:
            greet(device)

    @pl.when(jnp.logical_not(odd))
    def _():
        pl.semaphore_wait(barrier, len(near))
        for device in near:
            pl.semaphore_signal(answer, inc=1, device_id=device, device_id_type=MESH)

    def copy(src, dst, s, r, device):
        return pltpu.make_async_remote_copy(
            src_ref=src, dst_ref=dst, send_sem=s, recv_sem=r, device_id=device, device_id_type=MESH
        )

    hops = [k for k in range(1, layers)]
    hops = sorted(hops, key=lambda k: (k != layers // 2, k)) + [0]
    keepers = [lax.rem(z + k, layers) for k in hops]

    def group(g):
        return pl.ds(pl.multiple_of(keepers[g] * cw, cw), cw)

    own_panels = [col_hbm, row_hbm]
    to_y = [[copy(own_panels[k].at[:, group(g)], panels.at[k, 1, :, group(g)], ysend.at[k, g],
                  yrecv.at[k, g], (x, yq, z)) for k in range(2)] for g in range(layers)]
    to_sib = [copy(own_panels[k], panels.at[k, 0], ssend.at[k], srecv.at[k], (x, sib, z))
              for k in range(2)]
    onward = [[copy(panels.at[k, 1, :, group(g)], panels.at[k, 2, :, group(g)], fsend.at[k, g],
                    frecv.at[k, g], (x, sib, z)) for k in range(2)] for g in range(layers)]
    to_x = [
        copy(codes, codes_in, xsend.at[2], xrecv.at[2], (other, q, z)),
        copy(xs.at[:, pl.ds(0, tw)], xr, xsend.at[0], xrecv.at[0], (other, q, z)),
        copy(xs.at[:, pl.ds(tw, 4 * tw)], lhs.at[pl.ds(rows, rows), pl.ds(0, 4 * tw)],
             xsend.at[1], xrecv.at[1], (other, q, z)),
    ]

    def wide(a):
        return jnp.concatenate([a] * (tw // 128), axis=1)

    def flag(cond):
        return wide(cond.astype(jnp.float32).astype(jnp.bfloat16))

    def down(row):
        return jnp.transpose(jnp.broadcast_to(row.astype(jnp.float32), (128, rows)))

    @pl.when(odd)
    def _():
        pl.semaphore_wait(answer, len(near))

    for c in to_y[0] + to_sib:
        c.start()
    for g in range(1, layers):
        for c in to_y[g]:
            c.start()

    @pl.when(odd)
    def _():
        for n in range(layers):

            @pl.when(n != z)
            def _():
                greet((x, q, n))

    for c in loads[:3]:
        c.wait()
    dest = down(own[...]).astype(jnp.int32)
    dest_row = jnp.where(dest >= 4, 1, 0)
    dest_col = dest - 4 * dest_row
    here, there = flag(dest_row == x), flag(dest_row != x)

    def block(m):
        return amp[:, m * tw : (m + 1) * tw] * wide(down(mask[m : m + 1]).astype(jnp.bfloat16))

    codes[...] = jnp.broadcast_to(own[...] - 4 * jnp.where(own[...] >= 4, 1, 0), codes.shape).astype(
        jnp.float32
    ).astype(jnp.bfloat16)
    f32 = jnp.float32
    evens = (block(4).astype(f32) + block(6).astype(f32)).astype(jnp.bfloat16)
    odds = (block(5).astype(f32) + block(7).astype(f32)).astype(jnp.bfloat16)
    own_row = evens * here + odds * there
    xs[:, :tw] = odds * here + evens * there
    to_x[0].start()
    to_x[1].start()
    col_blocks = [block(s) for s in range(4)]
    for j in range(4):
        met = sum(col_blocks[s] * flag(dest_col == lax.rem(cols[j] + 4 - s, 4)) for s in range(4))
        lhs[:rows, j * tw : (j + 1) * tw] = met * here
        xs[:, (1 + j) * tw : (2 + j) * tw] = met * there

    to_x[2].start()

    for j in range(4):
        meets = flag(dest_col == cols[j])
        lhs[:rows, (4 + j) * tw : (5 + j) * tw] = own_row * meets

    def pass_on(g):
        for k in range(2):
            to_y[g][k].wait_recv()
            onward[g][k].start()

    for c in loads[3:]:
        c.wait()
    pass_on(0)
    for c in to_sib:
        c.wait_recv()
    for c in to_x:
        c.wait_recv()
    code = down(codes_in[...][:1])
    for j in range(4):
        meets = flag(code == cols[j].astype(jnp.float32))
        lhs[rows:, (4 + j) * tw : (5 + j) * tw] = xr[...] * meets

    def result(g, side):
        return copy(outb.at[side, g], inbox.at[side, g], osend.at[side, g], irecv.at[side, g],
                    (x if side == 0 else other, q, keepers[g]))

    for g in range(layers):
        if g + 1 < layers:
            pass_on(g + 1)
        total = jnp.zeros((2 * rows, cw), jnp.float32)
        for j in range(4):
            if j == 3:
                for k in range(2):
                    onward[g][k].wait_recv()
            col = colp[:, group(g)] if j == 0 else panels[0, j - 1, :, group(g)]
            row = rowp[:, group(g)] if j == 0 else panels[1, j - 1, :, group(g)]
            total += jnp.dot(lhs[:, j * tw : (j + 1) * tw], col, preferred_element_type=jnp.float32)
            total += jnp.dot(
                lhs[:, (4 + j) * tw : (5 + j) * tw], row, preferred_element_type=jnp.float32
            )
        outb[1, g] = total[rows:].astype(jnp.bfloat16)
        if g == 0:

            @pl.when(odd)
            def _():
                pl.semaphore_wait(barrier, layers - 1)
                pl.semaphore_signal(ready, inc=1, device_id=(other, q, z), device_id_type=MESH)

            @pl.when(jnp.logical_not(odd))
            def _():
                pl.semaphore_wait(ready, 1)

        result(g, 1).start()
        outb[0, g] = total[:rows].astype(jnp.bfloat16)
        if g < layers - 1:
            result(g, 0).start()

    kept = outb[0, layers - 1].astype(jnp.float32)
    for g in range(layers):
        if g < layers - 1:
            result(g, 0).wait_recv()
            kept += inbox[0, g].astype(jnp.float32)
        result(g, 1).wait_recv()
        kept += inbox[1, g].astype(jnp.float32)
    out[...] = kept.astype(out.dtype)

    for c in to_sib + to_x:
        c.wait_send()
    for g in range(layers):
        for c in to_y[g] + onward[g]:
            c.wait_send()
    for g in range(layers):
        result(g, 1).wait_send()
        if g < layers - 1:
            result(g, 0).wait_send()


def crossed(amplitudes, tile_mask, owners, col_panels, row_panels):
    layers = lax.axis_size("layer")
    rows, width_k = amplitudes.shape[2:]
    tw, nw = col_panels.shape[3:]
    blocks = tile_mask.shape[3]
    cw = nw // layers
    dma = pltpu.SemaphoreType.DMA
    bf16 = jnp.bfloat16
    vmem = pl.BlockSpec(memory_space=pltpu.VMEM)
    result = pl.pallas_call(
        functools.partial(kernel, layers),
        out_shape=jax.ShapeDtypeStruct((rows, cw), bf16),
        in_specs=[pl.BlockSpec(memory_space=pltpu.HBM)] * 5,
        out_specs=vmem,
        scratch_shapes=[
            pltpu.VMEM((rows, width_k), bf16),
            pltpu.VMEM((blocks, rows), jnp.int32),
            pltpu.VMEM((1, rows), jnp.int32),
            pltpu.VMEM((tw, nw), bf16),
            pltpu.VMEM((tw, nw), bf16),
            pltpu.VMEM((2, 3, tw, nw), bf16),
            pltpu.VMEM((2 * rows, 8 * tw), bf16),
            pltpu.VMEM((rows, 5 * tw), bf16),
            pltpu.VMEM((rows, tw), bf16),
            pltpu.VMEM((16, rows), bf16),
            pltpu.VMEM((16, rows), bf16),
            pltpu.VMEM((2, layers, rows, cw), bf16),
            pltpu.VMEM((2, layers, rows, cw), bf16),
            pltpu.SemaphoreType.REGULAR, pltpu.SemaphoreType.REGULAR,
            dma((5,)), dma((2, layers)), dma((2, layers)), dma((2,)), dma((2,)),
            dma((2, layers)), dma((2, layers)), dma((3,)), dma((3,)),
            dma((2, layers)), dma((2, layers)),
        ],
        compiler_params=pltpu.CompilerParams(
            collective_id=0, has_side_effects=True, vmem_limit_bytes=60 * 1024 * 1024
        ),
    )(
        amplitudes.reshape(rows, width_k),
        tile_mask.reshape(rows, blocks).T,
        owners.reshape(1, rows),
        col_panels.reshape(tw, nw),
        row_panels.reshape(tw, nw),
    )
    return result.reshape(1, 1, rows, cw)


def solution(mesh):
    small = mesh.shape["row"] == 2 and mesh.shape["col"] == 4
    return jax.shard_map(
        crossed if small else routed,
        mesh=mesh,
        in_specs=(
            P("row", "col", None, "layer"),
            P("row", "col", None, "layer"),
            P("row", "col", None, None),
            P("row", "col", "layer", None, None),
            P("row", "col", "layer", None, None),
        ),
        out_specs=P("row", "col", None, "layer"),
        check_vma=False,
    )
```
